32 devices in a mesh: dp: 4 (over y, x), seq: 8 (over z, core).
Axes of the slice: x: 2, y: 2, z: 4, core: 2. Of those that a mesh axis runs over, the one named last changes fastest.
Arguments:
- tokens: bfloat16 [4, 3072, 2048], P('dp', 'seq'), may hold values from -32 to 32
- w_qkv: bfloat16 [2048, 3072], P(('dp', 'seq')), may hold values from -1 to 1
- w_out: bfloat16 [1024, 2048], P(('dp', 'seq')), may hold values from -0.1875 to 0.1875
Outputs:
- mixed: bfloat16 [4, 3072, 2048], P('dp', 'seq')
The draws below stay inside these ranges and needn't reach their ends.
All inputs are finite; a program needn't handle non-finite values.
Results may differ from the reference program's by a relative error of at most 0.007.
Values may be sent and summed in bfloat16 or wider, within the bound.
A program may use at most 64 MiB of HBM per device.

```python
import math
import jax
import jax.numpy as jnp
from jax import lax

D = 2048
HEADS = 8
HEAD_DIM = 128
COLS = 96
BATCH = 4
GRID_ROWS = 32
TOKENS = 3072
INNER = 1024


def draw_tokens(key, part):
    keys = jax.random.split(jax.random.fold_in(key, 11), 6)
    values = jax.random.normal(keys[5], (BATCH, TOKENS, D))
    return jnp.clip(values, -32.0, 32.0).astype(jnp.bfloat16)


def draw_w_qkv(key, part):
    keys = jax.random.split(jax.random.fold_in(key, 23), 1)
    weights = jax.random.normal(keys[0], (D, HEADS, 3, HEAD_DIM)) / math.sqrt(D)
    return jnp.clip(weights.reshape(D, HEADS * 3 * HEAD_DIM), -1.0, 1.0).astype(jnp.bfloat16)


def block_scale(stream_key, dims, cuts, least, high):
    loudness = 1.0
    for axis_at, shards_of in cuts:
        heights = jax.random.uniform(jax.random.fold_in(jax.random.fold_in(stream_key, 6), axis_at), (shards_of,), jnp.float32, least / len(cuts), high / len(cuts))
        loudness = loudness * jnp.repeat(jnp.exp(heights), dims[axis_at] // shards_of).reshape((-1,) + (1,) * (len(dims) - 1 - axis_at))
    return loudness


def centred(rng, dims, width, reach, pieces=(), dtype=jnp.bfloat16):
    drawn = width * jax.random.normal(rng, dims, jnp.float32)
    if pieces:
        drawn = drawn * block_scale(rng, dims, pieces, -0.22, 0.18)
    return jnp.clip(drawn, -reach, reach).astype(dtype)


def setup_inputs(seed: int = 0) -> dict:
    key_of = jax.random.split(jax.random.key(seed), 4)
    tokens = draw_tokens(jax.random.fold_in(key_of[3], 71), 0)
    w_qkv = draw_w_qkv(jax.random.fold_in(key_of[3], 71), 0)
    w_out = centred(key_of[2], (INNER, D), INNER ** -0.5, 0.1875, ((0, 32),))
    return {"tokens": tokens, "w_qkv": w_qkv, "w_out": w_out}


def attend(query, keys, values, allowed):
    scores = jnp.einsum('bhqd,bhkd->bhqk', query.astype(jnp.float32), keys.astype(jnp.float32)) / math.sqrt(query.shape[-1])
    scores = jnp.where(allowed, scores, -jnp.inf)
    top = lax.optimization_barrier(jnp.max(scores, axis=-1, keepdims=True))
    expo = jnp.exp(scores - top)
    weights = (expo / lax.optimization_barrier(jnp.sum(expo, axis=-1, keepdims=True))).astype(jnp.bfloat16)
    return jnp.einsum('bhqk,bhkd->bhqd', weights.astype(jnp.float32), values.astype(jnp.float32)).astype(jnp.bfloat16)

def reference(tokens, w_qkv, w_out):
    half = HEADS // 2

    def one_sequence(sequence):
        qkv = jnp.dot(sequence, w_qkv, preferred_element_type=jnp.float32).astype(jnp.bfloat16)
        qkv = qkv.reshape(GRID_ROWS, COLS, HEADS, 3, HEAD_DIM)
        col_places = jnp.arange(COLS)
        row_places = jnp.arange(GRID_ROWS)
        row_mask = col_places[:, None] >= col_places[None, :]
        col_mask = row_places[:, None] >= row_places[None, :]
        row_part = jnp.transpose(qkv[:, :, :half], (0, 2, 3, 1, 4))
        row_out = attend(row_part[:, :, 0], row_part[:, :, 1], row_part[:, :, 2], row_mask)
        row_out = jnp.transpose(row_out, (0, 2, 1, 3))
        col_part = jnp.transpose(qkv[:, :, half:], (1, 2, 3, 0, 4))
        col_out = attend(col_part[:, :, 0], col_part[:, :, 1], col_part[:, :, 2], col_mask)
        col_out = jnp.transpose(col_out, (2, 0, 1, 3))
        heads_out = jnp.concatenate([row_out, col_out], axis=2).reshape(TOKENS, HEADS * HEAD_DIM)
        return jnp.dot(heads_out, w_out, preferred_element_type=jnp.float32).astype(jnp.bfloat16)
    return lax.map(one_sequence, tokens)
```

```python
import functools
import math

import jax
import jax.numpy as jnp
import numpy as np
from jax import lax
from jax.experimental import pallas as pl
from jax.experimental.pallas import tpu as pltpu
from jax.sharding import PartitionSpec as P

HEADS = 8
HEAD_DIM = 128
COLS = 96


def attend(query, keys, values, allowed):
    scores = jnp.einsum(
        "shqd,shkd->shqk", query, keys, preferred_element_type=jnp.float32
    ) / math.sqrt(query.shape[-1])
    scores = jnp.where(allowed, scores, -jnp.inf)
    top = jnp.max(scores, axis=-1, keepdims=True)
    expo = jnp.exp(scores - top)
    weights = (expo / jnp.sum(expo, axis=-1, keepdims=True)).astype(jnp.bfloat16)
    return jnp.einsum(
        "shqk,shkd->shqd", weights, values, preferred_element_type=jnp.float32
    ).astype(jnp.bfloat16)


def add_rows(left, piece):
    return jnp.dot(left, piece, preferred_element_type=jnp.float32)


def column_heads(packed):
    seq_count, grid_rows, local_cols, count, width = packed.shape
    length = grid_rows * local_cols
    flat = packed.reshape(seq_count, length, count, 3, width // 3)
    flat = jnp.transpose(flat, (0, 2, 3, 1, 4))
    places = jnp.arange(length)
    allowed = (places[:, None] % local_cols == places[None, :] % local_cols) & (
        places[:, None] >= places[None, :]
    )
    result = attend(flat[:, :, 0], flat[:, :, 1], flat[:, :, 2], allowed)
    result = jnp.transpose(result, (0, 2, 1, 3)).reshape(
        seq_count, grid_rows, local_cols, count, width // 3
    )
    return lax.all_to_all(result, "seq", split_axis=1, concat_axis=2, tiled=True)


def on_device(tokens, w_qkv, w_out):
    seq_count, tok_count, width = tokens.shape
    flat = tokens.reshape(seq_count * tok_count, width)
    half = HEADS // 2
    qkv = add_rows(flat, lax.all_gather(w_qkv, ("dp", "seq"), axis=0, tiled=True))
    qkv = qkv.astype(jnp.bfloat16).reshape(seq_count, tok_count, HEADS, 3, HEAD_DIM)
    col_packed = qkv[:, :, half:].reshape(seq_count, tok_count // COLS, COLS, half, 3 * HEAD_DIM)
    col_out = column_heads(
        lax.all_to_all(col_packed, "seq", split_axis=2, concat_axis=1, tiled=True)
    )
    col_out = col_out.reshape(seq_count, tok_count, half, HEAD_DIM)
    row_part = jnp.transpose(qkv[:, :, :half], (0, 2, 3, 1, 4))
    places = jnp.arange(tok_count)
    row_mask = (places[:, None] // COLS == places[None, :] // COLS) & (
        places[:, None] >= places[None, :]
    )
    row_out = attend(row_part[:, :, 0], row_part[:, :, 1], row_part[:, :, 2], row_mask)
    row_out = jnp.transpose(row_out, (0, 2, 1, 3))
    heads_out = jnp.concatenate([row_out, col_out], axis=2).reshape(
        seq_count * tok_count, HEADS * HEAD_DIM
    )
    mixed = add_rows(heads_out, lax.all_gather(w_out, ("dp", "seq"), axis=0, tiled=True))
    return mixed.astype(jnp.bfloat16).reshape(seq_count, tok_count, w_out.shape[1])


HALF = HEADS // 2
PACK = 3 * HEAD_DIM
OUT_CHUNKS = 4
JOBS = HEADS + OUT_CHUNKS
MESH = pl.DeviceIdType.MESH


def fused(tok_count, width, x_ref, wq_ref, wo_ref, perm_ref, unperm_ref, bias_ref, out_ref,
          xp, w, wo, qkv, col, col_out, home, heads,
          z_send, z_recv, f_send, f_recv, s_send, s_recv, c_send, c_recv,
          a_send, a_recv, b_send, b_recv):
    dp, seq = lax.axis_index("dp"), lax.axis_index("seq")
    y, x = dp // 2, dp % 2
    z, c = seq // 2, seq % 2
    dp_x, dp_y = 2 * y + (1 - x), 2 * (1 - y) + x
    share = tok_count // 8
    chunk = width // OUT_CHUNKS

    barrier = pltpu.get_barrier_semaphore()
    for step in range(1, 8):
        pl.semaphore_signal(barrier, inc=1, device_id=(dp, (seq + step) % 8), device_id_type=MESH)
    for other in (dp_x, dp_y):
        pl.semaphore_signal(barrier, inc=1, device_id=(other, seq), device_id_type=MESH)
    pl.semaphore_wait(barrier, 9)

    def send(source, target, s_sem, r_sem, device):
        return pltpu.make_async_remote_copy(
            src_ref=source, dst_ref=target, send_sem=s_sem, recv_sem=r_sem,
            device_id=device, device_id_type=MESH)

    def z_copies(own, full, rows, cols, k):
        return [send(own.at[:, cols], full.at[y, x, z, c, :, cols],
                     z_send.at[k, step - 1], z_recv.at[k, step - 1],
                     (dp, 2 * ((z + step) % 4) + c)) for step in range(1, 4)]

    def first_copies(own, full, rows, cols, k):
        low, high = pl.ds(0, rows // 2), pl.ds(rows // 2, rows // 2)
        to_x = full.at[y, x, :, c, low, cols]
        to_y = full.at[y, x, :, c, high, cols]
        return [send(to_x, to_x, f_send.at[k, 0], f_recv.at[k, 0], (dp_x, seq)),
                send(to_y, to_y, f_send.at[k, 1], f_recv.at[k, 1], (dp_y, seq))]

    def second_copies(own, full, rows, cols, k):
        low, high = pl.ds(0, rows // 2), pl.ds(rows // 2, rows // 2)
        to_y = full.at[y, :, :, c, low, cols]
        to_x = full.at[:, x, :, c, high, cols]
        return [send(to_y, to_y, s_send.at[k, 0], s_recv.at[k, 0], (dp_y, seq)),
                send(to_x, to_x, s_send.at[k, 1], s_recv.at[k, 1], (dp_x, seq))]

    def core_copies(own, full, rows, cols, k):
        part = full.at[:, :, :, c, :, cols]
        return [send(part, part, c_send.at[k], c_recv.at[k], (dp, 2 * z + (1 - c)))]

    def away_copies(k):
        copies = []
        for step in range(1, 8):
            peer = (seq + step) % 8
            copies.append(send(
                qkv.at[k, pl.ds(pl.multiple_of(peer * share, 16), share)],
                col.at[k, pl.ds(pl.multiple_of(seq * share, 16), share)],
                a_send.at[k, step - 1], a_recv.at[k, step - 1], (dp, peer)))
        return copies

    def back_copies(k):
        copies = []
        for step in range(1, 8):
            peer = (seq + step) % 8
            copies.append(send(
                col_out.at[k, pl.ds(pl.multiple_of(peer * share, 16), share)],
                home.at[k, pl.ds(pl.multiple_of(seq * share, 16), share)],
                b_send.at[k, step - 1], b_recv.at[k, step - 1], (dp, peer)))
        return copies

    def job(make, k, act):
        @pl.when((k >= 0) & (k < HEADS))
        def _():
            cols = pl.ds(pl.multiple_of(((k + HALF) % HEADS) * PACK, 128), PACK)
            for copy in make(wq_ref, w, wq_ref.shape[0], cols, k):
                act(copy)

        @pl.when((k >= HEADS) & (k < JOBS))
        def _():
            cols = pl.ds(pl.multiple_of((k - HEADS) * chunk, 128), chunk)
            for copy in make(wo_ref, wo, wo_ref.shape[0], cols, k):
                act(copy)

    def start(copy):
        copy.start()

    def arrived(copy):
        copy.wait_recv()

    def sent(copy):
        copy.wait_send()

    def attention(packed, bias):
        query, keys, values = (packed[:, p * HEAD_DIM:(p + 1) * HEAD_DIM] for p in range(3))
        scores = lax.dot_general(query, keys, (((1,), (1,)), ((), ())),
                                 preferred_element_type=jnp.float32)
        scores = scores * (1.0 / math.sqrt(HEAD_DIM)) + bias.astype(jnp.float32)
        expo = jnp.exp(scores - jnp.max(scores, axis=-1, keepdims=True))
        weights = expo * (1.0 / jnp.sum(expo, axis=-1, keepdims=True))
        return jnp.dot(weights.astype(jnp.bfloat16), values,
                       preferred_element_type=jnp.float32).astype(jnp.bfloat16)

    def reorder(order, block):
        return jnp.dot(order, block, preferred_element_type=jnp.float32).astype(jnp.bfloat16)

    job(z_copies, jnp.int32(0), start)
    w[y, x, z, c] = wq_ref[...]
    wo[y, x, z, c] = wo_ref[...]

    def permute(i, _):
        cols = pl.ds(pl.multiple_of(i * 512, 128), 512)
        xp[:, cols] = reorder(perm_ref[...], x_ref[:, cols])
        return 0

    lax.fori_loop(0, width // 512, permute, 0)

    def body(t, _):
        job(z_copies, t + 1, start)
        job(z_copies, jnp.where(t >= 1, t - 1, -1), arrived)
        job(first_copies, t - 1, start)
        job(first_copies, t - 2, arrived)
        job(second_copies, t - 2, start)
        job(second_copies, t - 3, arrived)
        job(core_copies, t - 3, start)
        job(core_copies, t - 4, arrived)
        k = t - 4

        @pl.when((k >= 0) & (k < HEADS))
        def _():
            cols = pl.ds(pl.multiple_of(((k + HALF) % HEADS) * PACK, 128), PACK)
            weight = w[:, :, :, :, :, cols].reshape(xp.shape[1], PACK)
            qkv[k] = jnp.dot(xp[...], weight,
                             preferred_element_type=jnp.float32).astype(jnp.bfloat16)

            @pl.when(k < HALF)
            def _():
                for copy in away_copies(k):
                    copy.start()
                mine = pl.ds(pl.multiple_of(seq * share, 16), share)
                col[k, mine] = qkv[k, mine]

            @pl.when(k >= HALF)
            def _():
                result = attention(qkv[k], bias_ref[0])
                heads[:, pl.ds(pl.multiple_of((k - HALF) * HEAD_DIM, 128), HEAD_DIM)] = reorder(
                    unperm_ref[...], result)

        a = t - 6

        @pl.when((a >= 0) & (a < HALF))
        def _():
            for copy in away_copies(a):
                copy.wait_recv()
            col_out[a] = attention(col[a], bias_ref[1])
            for copy in back_copies(a):
                copy.start()
            mine = pl.ds(pl.multiple_of(seq * share, 16), share)
            home[a, mine] = col_out[a, mine]

        b = t - 8

        @pl.when((b >= 0) & (b < HALF))
        def _():
            for copy in back_copies(b):
                copy.wait_recv()
            heads[:, pl.ds(pl.multiple_of((b + HALF) * HEAD_DIM, 128), HEAD_DIM)] = reorder(
                unperm_ref[...], home[b])

        @pl.when((k >= HEADS) & (k < JOBS))
        def _():
            cols = pl.ds(pl.multiple_of((k - HEADS) * chunk, 128), chunk)
            weight = wo[:, :, :, :, :, cols].reshape(heads.shape[1], chunk)
            out_ref[:, cols] = jnp.dot(heads[...], weight,
                                       preferred_element_type=jnp.float32).astype(jnp.bfloat16)
        return 0

    lax.fori_loop(0, JOBS + 4, body, 0)

    def drain(k, _):
        for make in (z_copies, first_copies, second_copies, core_copies):
            job(make, k, sent)
        return 0

    lax.fori_loop(0, JOBS, drain, 0)

    def drain_heads(k, _):
        for copy in away_copies(k) + back_copies(k):
            copy.wait_send()
        return 0

    lax.fori_loop(0, HALF, drain_heads, 0)


def on_torus(tokens, w_qkv, w_out):
    _, count, width = tokens.shape
    rows, share = count // COLS, COLS // 8
    places = np.arange(count).reshape(rows, 8, share).transpose(1, 0, 2).reshape(count)
    perm = (places[:, None] == np.arange(count)[None, :])
    later = np.arange(count)[:, None] >= np.arange(count)[None, :]
    in_row = (places // COLS)[:, None] == (places // COLS)[None, :]
    in_col = (np.arange(count) % share)[:, None] == (np.arange(count) % share)[None, :]
    bias = np.where(np.stack([in_row & later, in_col & later]), 0.0, -np.inf)
    bf16 = jnp.bfloat16
    inner = HEADS * HEAD_DIM
    vmem = pl.BlockSpec(memory_space=pltpu.VMEM)
    dma = pltpu.SemaphoreType.DMA
    out = pl.pallas_call(
        functools.partial(fused, count, width),
        out_shape=jax.ShapeDtypeStruct((count, width), bf16),
        in_specs=[vmem] * 6,
        out_specs=vmem,
        scratch_shapes=[
            pltpu.VMEM((count, width), bf16),
            pltpu.VMEM((2, 2, 4, 2) + w_qkv.shape, bf16),
            pltpu.VMEM((2, 2, 4, 2) + w_out.shape, bf16),
            pltpu.VMEM((HEADS, count, PACK), bf16),
            pltpu.VMEM((HALF, count, PACK), bf16),
            pltpu.VMEM((HALF, count, HEAD_DIM), bf16),
            pltpu.VMEM((HALF, count, HEAD_DIM), bf16),
            pltpu.VMEM((count, inner), bf16),
            dma((JOBS, 3)), dma((JOBS, 3)),
            dma((JOBS, 2)), dma((JOBS, 2)),
            dma((JOBS, 2)), dma((JOBS, 2)),
            dma((JOBS,)), dma((JOBS,)),
            dma((HALF, 7)), dma((HALF, 7)),
            dma((HALF, 7)), dma((HALF, 7)),
        ],
        compiler_params=pltpu.CompilerParams(
            collective_id=0, has_side_effects=True, vmem_limit_bytes=50 * 2**20),
        cost_estimate=pl.CostEstimate(
            flops=2 * count * width * (HEADS * PACK + inner),
            bytes_accessed=4 * count * width, transcendentals=HEADS * count * count),
    )(tokens.reshape(count, width), w_qkv, w_out, jnp.asarray(perm, bf16),
      jnp.asarray(perm.T, bf16), jnp.asarray(bias, bf16))
    return out.reshape(tokens.shape)


def solution(mesh):
    in_specs = (P("dp", "seq", None), P(("dp", "seq"), None), P(("dp", "seq"), None))
    out_specs = P("dp", "seq", None)
    fits = mesh.shape["dp"] == 4 and mesh.shape["seq"] == 8
    return jax.shard_map(
        on_torus if fits else on_device,
        mesh=mesh, in_specs=in_specs, out_specs=out_specs, check_vma=False
    )
```

```python
import functools
import math

import jax
import jax.numpy as jnp
import numpy as np
from jax import lax
from jax.experimental import pallas as pl
from jax.experimental.pallas import tpu as pltpu
from jax.sharding import PartitionSpec as P

HEADS = 8
HEAD_DIM = 128
COLS = 96


def attend(query, keys, values, allowed):
    scores = jnp.einsum(
        "shqd,shkd->shqk", query, keys, preferred_element_type=jnp.float32
    ) / math.sqrt(query.shape[-1])
    scores = jnp.where(allowed, scores, -jnp.inf)
    top = jnp.max(scores, axis=-1, keepdims=True)
    expo = jnp.exp(scores - top)
    weights = (expo / jnp.sum(expo, axis=-1, keepdims=True)).astype(jnp.bfloat16)
    return jnp.einsum(
        "shqk,shkd->shqd", weights, values, preferred_element_type=jnp.float32
    ).astype(jnp.bfloat16)


def add_rows(left, piece):
    return jnp.dot(left, piece, preferred_element_type=jnp.float32)


def column_heads(packed):
    seq_count, grid_rows, local_cols, count, width = packed.shape
    length = grid_rows * local_cols
    flat = packed.reshape(seq_count, length, count, 3, width // 3)
    flat = jnp.transpose(flat, (0, 2, 3, 1, 4))
    places = jnp.arange(length)
    allowed = (places[:, None] % local_cols == places[None, :] % local_cols) & (
        places[:, None] >= places[None, :]
    )
    result = attend(flat[:, :, 0], flat[:, :, 1], flat[:, :, 2], allowed)
    result = jnp.transpose(result, (0, 2, 1, 3)).reshape(
        seq_count, grid_rows, local_cols, count, width // 3
    )
    return lax.all_to_all(result, "seq", split_axis=1, concat_axis=2, tiled=True)


def on_device(tokens, w_qkv, w_out):
    seq_count, tok_count, width = tokens.shape
    flat = tokens.reshape(seq_count * tok_count, width)
    half = HEADS // 2
    qkv = add_rows(flat, lax.all_gather(w_qkv, ("dp", "seq"), axis=0, tiled=True))
    qkv = qkv.astype(jnp.bfloat16).reshape(seq_count, tok_count, HEADS, 3, HEAD_DIM)
    col_packed = qkv[:, :, half:].reshape(seq_count, tok_count // COLS, COLS, half, 3 * HEAD_DIM)
    col_out = column_heads(
        lax.all_to_all(col_packed, "seq", split_axis=2, concat_axis=1, tiled=True)
    )
    col_out = col_out.reshape(seq_count, tok_count, half, HEAD_DIM)
    row_part = jnp.transpose(qkv[:, :, :half], (0, 2, 3, 1, 4))
    places = jnp.arange(tok_count)
    row_mask = (places[:, None] // COLS == places[None, :] // COLS) & (
        places[:, None] >= places[None, :]
    )
    row_out = attend(row_part[:, :, 0], row_part[:, :, 1], row_part[:, :, 2], row_mask)
    row_out = jnp.transpose(row_out, (0, 2, 1, 3))
    heads_out = jnp.concatenate([row_out, col_out], axis=2).reshape(
        seq_count * tok_count, HEADS * HEAD_DIM
    )
    mixed = add_rows(heads_out, lax.all_gather(w_out, ("dp", "seq"), axis=0, tiled=True))
    return mixed.astype(jnp.bfloat16).reshape(seq_count, tok_count, w_out.shape[1])


HALF = HEADS // 2
PACK = 3 * HEAD_DIM
OUT_CHUNKS = 4
JOBS = HEADS + OUT_CHUNKS
MESH = pl.DeviceIdType.MESH


def fused(tok_count, width, x_hbm, wq_ref, wo_ref, perm_hbm, unperm_hbm, bias_hbm, out_ref,
          x_ref, perm_ref, unperm_ref, bias_ref, l_sem, xp, w, wo, qkv, col, col_out, home, heads,
          z_send, z_recv, f_send, f_recv, s_send, s_recv, c_send, c_recv,
          a_send, a_recv, b_send, b_recv):
    dp, seq = lax.axis_index("dp"), lax.axis_index("seq")
    y, x = dp // 2, dp % 2
    z, c = seq // 2, seq % 2
    dp_x, dp_y = 2 * y + (1 - x), 2 * (1 - y) + x
    share = tok_count // 8
    chunk = width // OUT_CHUNKS

    local = [pltpu.make_async_copy(source, target, l_sem.at[i]) for i, (source, target) in
             enumerate(((x_hbm, x_ref), (wq_ref, w.at[y, x, z, c]), (wo_ref, wo.at[y, x, z, c]),
                        (perm_hbm, perm_ref), (unperm_hbm, unperm_ref), (bias_hbm, bias_ref)))]
    for copy in local:
        copy.start()

    barrier = pltpu.get_barrier_semaphore()
    for step in range(1, 8):
        pl.semaphore_signal(barrier, inc=1, device_id=(dp, (seq + step) % 8), device_id_type=MESH)
    for other in (dp_x, dp_y):
        pl.semaphore_signal(barrier, inc=1, device_id=(other, seq), device_id_type=MESH)
    pl.semaphore_wait(barrier, 9)

    def send(source, target, s_sem, r_sem, device):
        return pltpu.make_async_remote_copy(
            src_ref=source, dst_ref=target, send_sem=s_sem, recv_sem=r_sem,
            device_id=device, device_id_type=MESH)

    def z_copies(hop, own, full, rows, cols, k):
        below, above = (z + 5 - hop) % 4, (z + hop - 1) % 4
        up, down = (z + 1) % 4, (z + 3) % 4
        copies = []
        for way, (block, target) in enumerate(((below, up), (above, down))):
            landing = full.at[y, x, block, c, :, cols]
            slot = 3 * way + hop - 1
            copies.append(send(own.at[:, cols] if hop == 1 else landing, landing,
                               z_send.at[k, slot], z_recv.at[k, slot], (dp, 2 * target + c)))
        return copies

    def z_sends(hop):
        return [(z < 3) & (z >= hop - 1), (z > 0) & (z <= 4 - hop)]

    def z_receives(hop):
        return [z >= hop, z <= 3 - hop]

    def z_job(hop, k, act, conditions):
        def guarded(own, full, rows, cols, k):
            return list(zip(conditions(hop), z_copies(hop, own, full, rows, cols, k)))

        def run(pair):
            condition, copy = pair

            @pl.when(condition)
            def _():
                act(copy)

        job(guarded, k, run)

    def first_copies(own, full, rows, cols, k):
        low, high = pl.ds(0, rows // 2), pl.ds(rows // 2, rows // 2)
        to_x = full.at[y, x, :, c, low, cols]
        to_y = full.at[y, x, :, c, high, cols]
        return [send(to_x, to_x, f_send.at[k, 0], f_recv.at[k, 0], (dp_x, seq)),
                send(to_y, to_y, f_send.at[k, 1], f_recv.at[k, 1], (dp_y, seq))]

    def second_copies(own, full, rows, cols, k):
        low, high = pl.ds(0, rows // 2), pl.ds(rows // 2, rows // 2)
        to_y = full.at[y, :, :, c, low, cols]
        to_x = full.at[:, x, :, c, high, cols]
        return [send(to_y, to_y, s_send.at[k, 0], s_recv.at[k, 0], (dp_y, seq)),
                send(to_x, to_x, s_send.at[k, 1], s_recv.at[k, 1], (dp_x, seq))]

    def core_copies(own, full, rows, cols, k):
        part = full.at[:, :, :, c, :, cols]
        return [send(part, part, c_send.at[k], c_recv.at[k], (dp, 2 * z + (1 - c)))]

    def away_copies(k):
        copies = []
        for step in range(1, 8):
            peer = (seq + step) % 8
            copies.append(send(
                qkv.at[k, pl.ds(pl.multiple_of(peer * share, 16), share)],
                col.at[k, pl.ds(pl.multiple_of(seq * share, 16), share)],
                a_send.at[k, step - 1], a_recv.at[k, step - 1], (dp, peer)))
        return copies

    def back_copies(k):
        copies = []
        for step in range(1, 8):
            peer = (seq + step) % 8
            copies.append(send(
                col_out.at[k, pl.ds(pl.multiple_of(peer * share, 16), share)],
                home.at[k, pl.ds(pl.multiple_of(seq * share, 16), share)],
                b_send.at[k, step - 1], b_recv.at[k, step - 1], (dp, peer)))
        return copies

    def job(make, k, act):
        @pl.when((k >= 0) & (k < HEADS))
        def _():
            cols = pl.ds(pl.multiple_of(((k + HALF) % HEADS) * PACK, 128), PACK)
            for copy in make(wq_ref, w, wq_ref.shape[0], cols, k):
                act(copy)

        @pl.when((k >= HEADS) & (k < JOBS))
        def _():
            cols = pl.ds(pl.multiple_of((k - HEADS) * chunk, 128), chunk)
            for copy in make(wo_ref, wo, wo_ref.shape[0], cols, k):
                act(copy)

    def start(copy):
        copy.start()

    def arrived(copy):
        copy.wait_recv()

    def sent(copy):
        copy.wait_send()

    def attention(packed, bias):
        query, keys, values = (packed[:, p * HEAD_DIM:(p + 1) * HEAD_DIM] for p in range(3))
        scores = lax.dot_general(query, keys, (((1,), (1,)), ((), ())),
                                 preferred_element_type=jnp.float32)
        scores = scores * (1.0 / math.sqrt(HEAD_DIM)) + bias.astype(jnp.float32)
        expo = jnp.exp(scores - jnp.max(scores, axis=-1, keepdims=True))
        weights = expo * (1.0 / jnp.sum(expo, axis=-1, keepdims=True))
        return jnp.dot(weights.astype(jnp.bfloat16), values,
                       preferred_element_type=jnp.float32).astype(jnp.bfloat16)

    def reorder(order, block):
        return jnp.dot(order, block, preferred_element_type=jnp.float32).astype(jnp.bfloat16)

    z_job(1, jnp.int32(0), start, z_sends)
    z_job(1, jnp.int32(1), start, z_sends)
    for copy in local:
        copy.wait()

    def permute(i, _):
        cols = pl.ds(pl.multiple_of(i * 512, 128), 512)
        xp[:, cols] = reorder(perm_ref[...], x_ref[:, cols])
        return 0

    z_job(1, jnp.int32(0), arrived, z_receives)
    z_job(2, jnp.int32(0), start, z_sends)
    lax.fori_loop(0, width // 512, permute, 0)

    def body(t, _):
        z_job(1, t + 2, start, z_sends)
        z_job(1, t + 1, arrived, z_receives)
        z_job(2, t + 1, start, z_sends)
        z_job(2, t, arrived, z_receives)
        z_job(3, t, start, z_sends)
        z_job(3, t - 1, arrived, z_receives)
        job(first_copies, t - 1, start)
        job(first_copies, t - 2, arrived)
        job(second_copies, t - 2, start)
        job(second_copies, t - 3, arrived)
        job(core_copies, t - 3, start)
        job(core_copies, t - 4, arrived)
        k = t - 4

        @pl.when((k >= 0) & (k < HEADS))
        def _():
            cols = pl.ds(pl.multiple_of(((k + HALF) % HEADS) * PACK, 128), PACK)
            weight = w[:, :, :, :, :, cols].reshape(xp.shape[1], PACK)
            qkv[k] = jnp.dot(xp[...], weight,
                             preferred_element_type=jnp.float32).astype(jnp.bfloat16)

            @pl.when(k < HALF)
            def _():
                for copy in away_copies(k):
                    copy.start()
                mine = pl.ds(pl.multiple_of(seq * share, 16), share)
                col[k, mine] = qkv[k, mine]

            @pl.when(k >= HALF)
            def _():
                result = attention(qkv[k], bias_ref[0])
                heads[:, pl.ds(pl.multiple_of((k - HALF) * HEAD_DIM, 128), HEAD_DIM)] = reorder(
                    unperm_ref[...], result)

        a = t - 6

        @pl.when((a >= 0) & (a < HALF))
        def _():
            for copy in away_copies(a):
                copy.wait_recv()
            col_out[a] = attention(col[a], bias_ref[1])
            for copy in back_copies(a):
                copy.start()
            mine = pl.ds(pl.multiple_of(seq * share, 16), share)
            home[a, mine] = col_out[a, mine]

        b = t - 8

        @pl.when((b >= 0) & (b < HALF))
        def _():
            for copy in back_copies(b):
                copy.wait_recv()
            heads[:, pl.ds(pl.multiple_of((b + HALF) * HEAD_DIM, 128), HEAD_DIM)] = reorder(
                unperm_ref[...], home[b])

        @pl.when((k >= HEADS) & (k < JOBS))
        def _():
            cols = pl.ds(pl.multiple_of((k - HEADS) * chunk, 128), chunk)
            weight = wo[:, :, :, :, :, cols].reshape(heads.shape[1], chunk)
            out_ref[:, cols] = jnp.dot(heads[...], weight,
                                       preferred_element_type=jnp.float32).astype(jnp.bfloat16)
        return 0

    lax.fori_loop(0, JOBS + 4, body, 0)

    def drain(k, _):
        for hop in (1, 2, 3):
            z_job(hop, k, sent, z_sends)
        for make in (first_copies, second_copies, core_copies):
            job(make, k, sent)
        return 0

    lax.fori_loop(0, JOBS, drain, 0)

    def drain_heads(k, _):
        for copy in away_copies(k) + back_copies(k):
            copy.wait_send()
        return 0

    lax.fori_loop(0, HALF, drain_heads, 0)


def on_torus(tokens, w_qkv, w_out):
    _, count, width = tokens.shape
    rows, share = count // COLS, COLS // 8
    places = np.arange(count).reshape(rows, 8, share).transpose(1, 0, 2).reshape(count)
    perm = (places[:, None] == np.arange(count)[None, :])
    later = np.arange(count)[:, None] >= np.arange(count)[None, :]
    in_row = (places // COLS)[:, None] == (places // COLS)[None, :]
    in_col = (np.arange(count) % share)[:, None] == (np.arange(count) % share)[None, :]
    bias = np.where(np.stack([in_row & later, in_col & later]), 0.0, -np.inf)
    bf16 = jnp.bfloat16
    inner = HEADS * HEAD_DIM
    vmem = pl.BlockSpec(memory_space=pltpu.VMEM)
    dma = pltpu.SemaphoreType.DMA
    out = pl.pallas_call(
        functools.partial(fused, count, width),
        out_shape=jax.ShapeDtypeStruct((count, width), bf16),
        in_specs=[pl.BlockSpec(memory_space=pltpu.HBM)] * 6,
        out_specs=vmem,
        scratch_shapes=[
            pltpu.VMEM((count, width), bf16),
            pltpu.VMEM((count, count), bf16),
            pltpu.VMEM((count, count), bf16),
            pltpu.VMEM((2, count, count), bf16),
            dma((6,)),
            pltpu.VMEM((count, width), bf16),
            pltpu.VMEM((2, 2, 4, 2) + w_qkv.shape, bf16),
            pltpu.VMEM((2, 2, 4, 2) + w_out.shape, bf16),
            pltpu.VMEM((HEADS, count, PACK), bf16),
            pltpu.VMEM((HALF, count, PACK), bf16),
            pltpu.VMEM((HALF, count, HEAD_DIM), bf16),
            pltpu.VMEM((HALF, count, HEAD_DIM), bf16),
            pltpu.VMEM((count, inner), bf16),
            dma((JOBS, 6)), dma((JOBS, 6)),
            dma((JOBS, 2)), dma((JOBS, 2)),
            dma((JOBS, 2)), dma((JOBS, 2)),
            dma((JOBS,)), dma((JOBS,)),
            dma((HALF, 7)), dma((HALF, 7)),
            dma((HALF, 7)), dma((HALF, 7)),
        ],
        compiler_params=pltpu.CompilerParams(
            collective_id=0, has_side_effects=True, vmem_limit_bytes=62 * 2**20),
        cost_estimate=pl.CostEstimate(
            flops=2 * count * width * (HEADS * PACK + inner),
            bytes_accessed=4 * count * width, transcendentals=HEADS * count * count),
    )(tokens.reshape(count, width), w_qkv, w_out, jnp.asarray(perm, bf16),
      jnp.asarray(perm.T, bf16), jnp.asarray(bias, bf16))
    return out.reshape(tokens.shape)


def solution(mesh):
    in_specs = (P("dp", "seq", None), P(("dp", "seq"), None), P(("dp", "seq"), None))
    out_specs = P("dp", "seq", None)
    fits = mesh.shape["dp"] == 4 and mesh.shape["seq"] == 8
    return jax.shard_map(
        on_torus if fits else on_device,
        mesh=mesh, in_specs=in_specs, out_specs=out_specs, check_vma=False
    )
```

```python
import functools
import math

import jax
import jax.numpy as jnp
import numpy as np
from jax import lax
from jax.experimental import pallas as pl
from jax.experimental.pallas import tpu as pltpu
from jax.sharding import PartitionSpec as P

HEADS = 8
HEAD_DIM = 128
COLS = 96


def attend(query, keys, values, allowed):
    scores = jnp.einsum(
        "shqd,shkd->shqk", query, keys, preferred_element_type=jnp.float32
    ) / math.sqrt(query.shape[-1])
    scores = jnp.where(allowed, scores, -jnp.inf)
    top = jnp.max(scores, axis=-1, keepdims=True)
    expo = jnp.exp(scores - top)
    weights = (expo / jnp.sum(expo, axis=-1, keepdims=True)).astype(jnp.bfloat16)
    return jnp.einsum(
        "shqk,shkd->shqd", weights, values, preferred_element_type=jnp.float32
    ).astype(jnp.bfloat16)


def add_rows(left, piece):
    return jnp.dot(left, piece, preferred_element_type=jnp.float32)


def column_heads(packed):
    seq_count, grid_rows, local_cols, count, width = packed.shape
    length = grid_rows * local_cols
    flat = packed.reshape(seq_count, length, count, 3, width // 3)
    flat = jnp.transpose(flat, (0, 2, 3, 1, 4))
    places = jnp.arange(length)
    allowed = (places[:, None] % local_cols == places[None, :] % local_cols) & (
        places[:, None] >= places[None, :]
    )
    result = attend(flat[:, :, 0], flat[:, :, 1], flat[:, :, 2], allowed)
    result = jnp.transpose(result, (0, 2, 1, 3)).reshape(
        seq_count, grid_rows, local_cols, count, width // 3
    )
    return lax.all_to_all(result, "seq", split_axis=1, concat_axis=2, tiled=True)


def on_device(tokens, w_qkv, w_out):
    seq_count, tok_count, width = tokens.shape
    flat = tokens.reshape(seq_count * tok_count, width)
    half = HEADS // 2
    qkv = add_rows(flat, lax.all_gather(w_qkv, ("dp", "seq"), axis=0, tiled=True))
    qkv = qkv.astype(jnp.bfloat16).reshape(seq_count, tok_count, HEADS, 3, HEAD_DIM)
    col_packed = qkv[:, :, half:].reshape(seq_count, tok_count // COLS, COLS, half, 3 * HEAD_DIM)
    col_out = column_heads(
        lax.all_to_all(col_packed, "seq", split_axis=2, concat_axis=1, tiled=True)
    )
    col_out = col_out.reshape(seq_count, tok_count, half, HEAD_DIM)
    row_part = jnp.transpose(qkv[:, :, :half], (0, 2, 3, 1, 4))
    places = jnp.arange(tok_count)
    row_mask = (places[:, None] // COLS == places[None, :] // COLS) & (
        places[:, None] >= places[None, :]
    )
    row_out = attend(row_part[:, :, 0], row_part[:, :, 1], row_part[:, :, 2], row_mask)
    row_out = jnp.transpose(row_out, (0, 2, 1, 3))
    heads_out = jnp.concatenate([row_out, col_out], axis=2).reshape(
        seq_count * tok_count, HEADS * HEAD_DIM
    )
    mixed = add_rows(heads_out, lax.all_gather(w_out, ("dp", "seq"), axis=0, tiled=True))
    return mixed.astype(jnp.bfloat16).reshape(seq_count, tok_count, w_out.shape[1])


HALF = HEADS // 2
PACK = 3 * HEAD_DIM
OUT_CHUNKS = 4
JOBS = HEADS + OUT_CHUNKS
MESH = pl.DeviceIdType.MESH


def fused(tok_count, width, x_hbm, wq_ref, wo_ref, perm_hbm, unperm_hbm, bias_hbm, out_ref,
          x_ref, perm_ref, unperm_ref, bias_ref, l_sem, xp, w, wo, qkv, col, col_out, home, heads,
          z_send, z_recv, f_send, f_recv, s_send, s_recv, c_send, c_recv,
          a_send, a_recv, b_send, b_recv):
    dp, seq = lax.axis_index("dp"), lax.axis_index("seq")
    y, x = dp // 2, dp % 2
    z, c = seq // 2, seq % 2
    dp_x, dp_y = 2 * y + (1 - x), 2 * (1 - y) + x
    share = tok_count // 8
    chunk = width // OUT_CHUNKS

    local = [pltpu.make_async_copy(source, target, l_sem.at[i]) for i, (source, target) in
             enumerate(((x_hbm, x_ref), (wq_ref, w.at[y, x, z, c]), (wo_ref, wo.at[y, x, z, c]),
                        (perm_hbm, perm_ref), (unperm_hbm, unperm_ref), (bias_hbm, bias_ref)))]
    for copy in local:
        copy.start()

    barrier = pltpu.get_barrier_semaphore()
    for step in range(1, 8):
        pl.semaphore_signal(barrier, inc=1, device_id=(dp, (seq + step) % 8), device_id_type=MESH)
    for other in (dp_x, dp_y):
        pl.semaphore_signal(barrier, inc=1, device_id=(other, seq), device_id_type=MESH)
    pl.semaphore_wait(barrier, 9)

    def send(source, target, s_sem, r_sem, device):
        return pltpu.make_async_remote_copy(
            src_ref=source, dst_ref=target, send_sem=s_sem, recv_sem=r_sem,
            device_id=device, device_id_type=MESH)

    def z_copies(hop, own, full, rows, cols, k):
        below, above = (z + 5 - hop) % 4, (z + hop - 1) % 4
        up, down = (z + 1) % 4, (z + 3) % 4
        copies = []
        for way, (block, target) in enumerate(((below, up), (above, down))):
            landing = full.at[y, x, block, c, :, cols]
            slot = 3 * way + hop - 1
            copies.append(send(own.at[:, cols] if hop == 1 else landing, landing,
                               z_send.at[k, slot], z_recv.at[k, slot], (dp, 2 * target + c)))
        return copies

    def z_sends(hop):
        return [(z < 3) & (z >= hop - 1), (z > 0) & (z <= 4 - hop)]

    def z_receives(hop):
        return [z >= hop, z <= 3 - hop]

    def z_job(hop, k, act, conditions):
        def guarded(own, full, rows, cols, k):
            return list(zip(conditions(hop), z_copies(hop, own, full, rows, cols, k)))

        def run(pair):
            condition, copy = pair

            @pl.when(condition)
            def _():
                act(copy)

        job(guarded, k, run)

    def first_copies(own, full, rows, cols, k):
        low, high = pl.ds(0, rows // 2), pl.ds(rows // 2, rows // 2)
        to_x = full.at[y, x, :, c, low, cols]
        to_y = full.at[y, x, :, c, high, cols]
        return [send(to_x, to_x, f_send.at[k, 0], f_recv.at[k, 0], (dp_x, seq)),
                send(to_y, to_y, f_send.at[k, 1], f_recv.at[k, 1], (dp_y, seq))]

    def second_copies(own, full, rows, cols, k):
        low, high = pl.ds(0, rows // 2), pl.ds(rows // 2, rows // 2)
        to_y = full.at[y, :, :, c, low, cols]
        to_x = full.at[:, x, :, c, high, cols]
        return [send(to_y, to_y, s_send.at[k, 0], s_recv.at[k, 0], (dp_y, seq)),
                send(to_x, to_x, s_send.at[k, 1], s_recv.at[k, 1], (dp_x, seq))]

    def core_copies(own, full, rows, cols, k):
        part = full.at[:, :, :, c, :, cols]
        return [send(part, part, c_send.at[k], c_recv.at[k], (dp, 2 * z + (1 - c)))]

    def away_copies(k):
        copies = []
        for step in range(1, 8):
            peer = (seq + step) % 8
            copies.append(send(
                qkv.at[k, pl.ds(pl.multiple_of(peer * share, 16), share)],
                col.at[k, pl.ds(pl.multiple_of(seq * share, 16), share)],
                a_send.at[k, step - 1], a_recv.at[k, step - 1], (dp, peer)))
        return copies

    def back_copies(k):
        copies = []
        for step in range(1, 8):
            peer = (seq + step) % 8
            copies.append(send(
                col_out.at[k, pl.ds(pl.multiple_of(peer * share, 16), share)],
                home.at[k, pl.ds(pl.multiple_of(seq * share, 16), share)],
                b_send.at[k, step - 1], b_recv.at[k, step - 1], (dp, peer)))
        return copies

    def job(make, k, act):
        @pl.when((k >= 0) & (k < HEADS))
        def _():
            cols = pl.ds(pl.multiple_of(((k + HALF) % HEADS) * PACK, 128), PACK)
            for copy in make(wq_ref, w, wq_ref.shape[0], cols, k):
                act(copy)

        @pl.when((k >= HEADS) & (k < JOBS))
        def _():
            cols = pl.ds(pl.multiple_of((k - HEADS) * chunk, 128), chunk)
            for copy in make(wo_ref, wo, wo_ref.shape[0], cols, k):
                act(copy)

    def start(copy):
        copy.start()

    def arrived(copy):
        copy.wait_recv()

    def sent(copy):
        copy.wait_send()

    def attention(packed, bias):
        query, keys, values = (packed[:, p * HEAD_DIM:(p + 1) * HEAD_DIM] for p in range(3))
        scores = lax.dot_general(query, keys, (((1,), (1,)), ((), ())),
                                 preferred_element_type=jnp.float32)
        scores = scores * (1.0 / math.sqrt(HEAD_DIM)) + bias.astype(jnp.float32)
        expo = jnp.exp(scores - jnp.max(scores, axis=-1, keepdims=True))
        weights = expo * (1.0 / jnp.sum(expo, axis=-1, keepdims=True))
        return jnp.dot(weights.astype(jnp.bfloat16), values,
                       preferred_element_type=jnp.float32).astype(jnp.bfloat16)

    def reorder(order, block):
        return jnp.dot(order, block, preferred_element_type=jnp.float32).astype(jnp.bfloat16)

    def z_ahead(t):
        z_job(1, t + 3, start, z_sends)
        z_job(1, t + 2, arrived, z_receives)
        z_job(2, t + 2, start, z_sends)
        z_job(2, t + 1, arrived, z_receives)
        z_job(3, t + 1, start, z_sends)

    z_job(1, jnp.int32(0), start, z_sends)
    z_job(1, jnp.int32(1), start, z_sends)
    for copy in local:
        copy.wait()

    def permute(i, _):
        cols = pl.ds(pl.multiple_of(i * 512, 128), 512)
        xp[:, cols] = reorder(perm_ref[...], x_ref[:, cols])
        return 0

    z_job(1, jnp.int32(0), arrived, z_receives)
    z_job(2, jnp.int32(0), start, z_sends)
    z_job(1, jnp.int32(2), start, z_sends)
    z_job(1, jnp.int32(1), arrived, z_receives)
    z_job(2, jnp.int32(1), start, z_sends)
    z_job(2, jnp.int32(0), arrived, z_receives)
    z_job(3, jnp.int32(0), start, z_sends)
    lax.fori_loop(0, width // 512, permute, 0)

    def body(t, _):
        z_job(3, t - 1, arrived, z_receives)
        job(first_copies, t - 1, start)
        job(first_copies, t - 2, arrived)
        job(second_copies, t - 2, start)
        job(second_copies, t - 4, arrived)
        job(core_copies, t - 4, start)
        z_ahead(t)
        job(core_copies, t - 5, arrived)
        k = t - 5

        @pl.when((k >= 0) & (k < HEADS))
        def _():
            cols = pl.ds(pl.multiple_of(((k + HALF) % HEADS) * PACK, 128), PACK)
            weight = w[:, :, :, :, :, cols].reshape(xp.shape[1], PACK)
            qkv[k] = jnp.dot(xp[...], weight,
                             preferred_element_type=jnp.float32).astype(jnp.bfloat16)

            @pl.when(k < HALF)
            def _():
                for copy in away_copies(k):
                    copy.start()
                mine = pl.ds(pl.multiple_of(seq * share, 16), share)
                col[k, mine] = qkv[k, mine]

            @pl.when(k >= HALF)
            def _():
                result = attention(qkv[k], bias_ref[0])
                heads[:, pl.ds(pl.multiple_of((k - HALF) * HEAD_DIM, 128), HEAD_DIM)] = reorder(
                    unperm_ref[...], result)

        a = t - 7

        @pl.when((a >= 0) & (a < HALF))
        def _():
            for copy in away_copies(a):
                copy.wait_recv()
            col_out[a] = attention(col[a], bias_ref[1])
            for copy in back_copies(a):
                copy.start()
            mine = pl.ds(pl.multiple_of(seq * share, 16), share)
            home[a, mine] = col_out[a, mine]

        b = t - 9

        @pl.when((b >= 0) & (b < HALF))
        def _():
            for copy in back_copies(b):
                copy.wait_recv()
            heads[:, pl.ds(pl.multiple_of((b + HALF) * HEAD_DIM, 128), HEAD_DIM)] = reorder(
                unperm_ref[...], home[b])

        @pl.when((k >= HEADS) & (k < JOBS))
        def _():
            cols = pl.ds(pl.multiple_of((k - HEADS) * chunk, 128), chunk)
            weight = wo[:, :, :, :, :, cols].reshape(heads.shape[1], chunk)
            out_ref[:, cols] = jnp.dot(heads[...], weight,
                                       preferred_element_type=jnp.float32).astype(jnp.bfloat16)
        return 0

    lax.fori_loop(0, JOBS + 5, body, 0)

    def drain(k, _):
        for hop in (1, 2, 3):
            z_job(hop, k, sent, z_sends)
        for make in (first_copies, second_copies, core_copies):
            job(make, k, sent)
        return 0

    lax.fori_loop(0, JOBS, drain, 0)

    def drain_heads(k, _):
        for copy in away_copies(k) + back_copies(k):
            copy.wait_send()
        return 0

    lax.fori_loop(0, HALF, drain_heads, 0)


def on_torus(tokens, w_qkv, w_out):
    _, count, width = tokens.shape
    rows, share = count // COLS, COLS // 8
    places = np.arange(count).reshape(rows, 8, share).transpose(1, 0, 2).reshape(count)
    perm = (places[:, None] == np.arange(count)[None, :])
    later = np.arange(count)[:, None] >= np.arange(count)[None, :]
    in_row = (places // COLS)[:, None] == (places // COLS)[None, :]
    in_col = (np.arange(count) % share)[:, None] == (np.arange(count) % share)[None, :]
    bias = np.where(np.stack([in_row & later, in_col & later]), 0.0, -np.inf)
    bf16 = jnp.bfloat16
    inner = HEADS * HEAD_DIM
    vmem = pl.BlockSpec(memory_space=pltpu.VMEM)
    dma = pltpu.SemaphoreType.DMA
    out = pl.pallas_call(
        functools.partial(fused, count, width),
        out_shape=jax.ShapeDtypeStruct((count, width), bf16),
        in_specs=[pl.BlockSpec(memory_space=pltpu.HBM)] * 6,
        out_specs=vmem,
        scratch_shapes=[
            pltpu.VMEM((count, width), bf16),
            pltpu.VMEM((count, count), bf16),
            pltpu.VMEM((count, count), bf16),
            pltpu.VMEM((2, count, count), bf16),
            dma((6,)),
            pltpu.VMEM((count, width), bf16),
            pltpu.VMEM((2, 2, 4, 2) + w_qkv.shape, bf16),
            pltpu.VMEM((2, 2, 4, 2) + w_out.shape, bf16),
            pltpu.VMEM((HEADS, count, PACK), bf16),
            pltpu.VMEM((HALF, count, PACK), bf16),
            pltpu.VMEM((HALF, count, HEAD_DIM), bf16),
            pltpu.VMEM((HALF, count, HEAD_DIM), bf16),
            pltpu.VMEM((count, inner), bf16),
            dma((JOBS, 6)), dma((JOBS, 6)),
            dma((JOBS, 2)), dma((JOBS, 2)),
            dma((JOBS, 2)), dma((JOBS, 2)),
            dma((JOBS,)), dma((JOBS,)),
            dma((HALF, 7)), dma((HALF, 7)),
            dma((HALF, 7)), dma((HALF, 7)),
        ],
        compiler_params=pltpu.CompilerParams(
            collective_id=0, has_side_effects=True, vmem_limit_bytes=62 * 2**20),
        cost_estimate=pl.CostEstimate(
            flops=2 * count * width * (HEADS * PACK + inner),
            bytes_accessed=4 * count * width, transcendentals=HEADS * count * count),
    )(tokens.reshape(count, width), w_qkv, w_out, jnp.asarray(perm, bf16),
      jnp.asarray(perm.T, bf16), jnp.asarray(bias, bf16))
    return out.reshape(tokens.shape)


def solution(mesh):
    in_specs = (P("dp", "seq", None), P(("dp", "seq"), None), P(("dp", "seq"), None))
    out_specs = P("dp", "seq", None)
    fits = mesh.shape["dp"] == 4 and mesh.shape["seq"] == 8
    return jax.shard_map(
        on_torus if fits else on_device,
        mesh=mesh, in_specs=in_specs, out_specs=out_specs, check_vma=False
    )
```

```python
import functools
import math

import jax
import jax.numpy as jnp
import numpy as np
from jax import lax
from jax.experimental import pallas as pl
from jax.experimental.pallas import tpu as pltpu
from jax.sharding import PartitionSpec as P

HEADS = 8
HEAD_DIM = 128
COLS = 96


def attend(query, keys, values, allowed):
    scores = jnp.einsum(
        "shqd,shkd->shqk", query, keys, preferred_element_type=jnp.float32
    ) / math.sqrt(query.shape[-1])
    scores = jnp.where(allowed, scores, -jnp.inf)
    top = jnp.max(scores, axis=-1, keepdims=True)
    expo = jnp.exp(scores - top)
    weights = (expo / jnp.sum(expo, axis=-1, keepdims=True)).astype(jnp.bfloat16)
    return jnp.einsum(
        "shqk,shkd->shqd", weights, values, preferred_element_type=jnp.float32
    ).astype(jnp.bfloat16)


def add_rows(left, piece):
    return jnp.dot(left, piece, preferred_element_type=jnp.float32)


def column_heads(packed):
    seq_count, grid_rows, local_cols, count, width = packed.shape
    length = grid_rows * local_cols
    flat = packed.reshape(seq_count, length, count, 3, width // 3)
    flat = jnp.transpose(flat, (0, 2, 3, 1, 4))
    places = jnp.arange(length)
    allowed = (places[:, None] % local_cols == places[None, :] % local_cols) & (
        places[:, None] >= places[None, :]
    )
    result = attend(flat[:, :, 0], flat[:, :, 1], flat[:, :, 2], allowed)
    result = jnp.transpose(result, (0, 2, 1, 3)).reshape(
        seq_count, grid_rows, local_cols, count, width // 3
    )
    return lax.all_to_all(result, "seq", split_axis=1, concat_axis=2, tiled=True)


def on_device(tokens, w_qkv, w_out):
    seq_count, tok_count, width = tokens.shape
    flat = tokens.reshape(seq_count * tok_count, width)
    half = HEADS // 2
    qkv = add_rows(flat, lax.all_gather(w_qkv, ("dp", "seq"), axis=0, tiled=True))
    qkv = qkv.astype(jnp.bfloat16).reshape(seq_count, tok_count, HEADS, 3, HEAD_DIM)
    col_packed = qkv[:, :, half:].reshape(seq_count, tok_count // COLS, COLS, half, 3 * HEAD_DIM)
    col_out = column_heads(
        lax.all_to_all(col_packed, "seq", split_axis=2, concat_axis=1, tiled=True)
    )
    col_out = col_out.reshape(seq_count, tok_count, half, HEAD_DIM)
    row_part = jnp.transpose(qkv[:, :, :half], (0, 2, 3, 1, 4))
    places = jnp.arange(tok_count)
    row_mask = (places[:, None] // COLS == places[None, :] // COLS) & (
        places[:, None] >= places[None, :]
    )
    row_out = attend(row_part[:, :, 0], row_part[:, :, 1], row_part[:, :, 2], row_mask)
    row_out = jnp.transpose(row_out, (0, 2, 1, 3))
    heads_out = jnp.concatenate([row_out, col_out], axis=2).reshape(
        seq_count * tok_count, HEADS * HEAD_DIM
    )
    mixed = add_rows(heads_out, lax.all_gather(w_out, ("dp", "seq"), axis=0, tiled=True))
    return mixed.astype(jnp.bfloat16).reshape(seq_count, tok_count, w_out.shape[1])


HALF = HEADS // 2
PACK = 3 * HEAD_DIM
OUT_CHUNKS = 4
JOBS = HEADS + OUT_CHUNKS
MESH = pl.DeviceIdType.MESH


def fused(tok_count, width, x_hbm, wq_ref, wo_ref, perm_hbm, unperm_hbm, bias_hbm, out_ref,
          x_ref, perm_ref, unperm_ref, bias_ref, l_sem, xp, w, wo, qkv, col, col_out, home, heads,
          z_send, z_recv, f_send, f_recv, s_send, s_recv, c_send, c_recv,
          a_send, a_recv, b_send, b_recv):
    dp, seq = lax.axis_index("dp"), lax.axis_index("seq")
    y, x = dp // 2, dp % 2
    z, c = seq // 2, seq % 2
    dp_x, dp_y = 2 * y + (1 - x), 2 * (1 - y) + x
    share = tok_count // 8
    chunk = width // OUT_CHUNKS

    local = [pltpu.make_async_copy(source, target, l_sem.at[i]) for i, (source, target) in
             enumerate(((x_hbm, x_ref), (wq_ref, w.at[y, x, z, c]), (wo_ref, wo.at[y, x, z, c]),
                        (perm_hbm, perm_ref), (unperm_hbm, unperm_ref), (bias_hbm, bias_ref)))]
    for copy in local:
        copy.start()

    barrier = pltpu.get_barrier_semaphore()
    for step in range(1, 8):
        pl.semaphore_signal(barrier, inc=1, device_id=(dp, (seq + step) % 8), device_id_type=MESH)
    for other in (dp_x, dp_y):
        pl.semaphore_signal(barrier, inc=1, device_id=(other, seq), device_id_type=MESH)
    pl.semaphore_wait(barrier, 9)

    def send(source, target, s_sem, r_sem, device):
        return pltpu.make_async_remote_copy(
            src_ref=source, dst_ref=target, send_sem=s_sem, recv_sem=r_sem,
            device_id=device, device_id_type=MESH)

    def z_copies(hop, own, full, rows, cols, k):
        below, above = (z + 5 - hop) % 4, (z + hop - 1) % 4
        up, down = (z + 1) % 4, (z + 3) % 4
        copies = []
        for way, (block, target) in enumerate(((below, up), (above, down))):
            landing = full.at[y, x, block, c, :, cols]
            slot = 3 * way + hop - 1
            copies.append(send(own.at[:, cols] if hop == 1 else landing, landing,
                               z_send.at[k, slot], z_recv.at[k, slot], (dp, 2 * target + c)))
        return copies

    def z_sends(hop):
        return [(z < 3) & (z >= hop - 1), (z > 0) & (z <= 4 - hop)]

    def z_receives(hop):
        return [z >= hop, z <= 3 - hop]

    def z_job(hop, k, act, conditions):
        def guarded(own, full, rows, cols, k):
            return list(zip(conditions(hop), z_copies(hop, own, full, rows, cols, k)))

        def run(pair):
            condition, copy = pair

            @pl.when(condition)
            def _():
                act(copy)

        job(guarded, k, run)

    def first_copies(own, full, rows, cols, k):
        low, high = pl.ds(0, rows // 2), pl.ds(rows // 2, rows // 2)
        to_x = full.at[y, x, :, c, low, cols]
        to_y = full.at[y, x, :, c, high, cols]
        return [send(to_x, to_x, f_send.at[k, 0], f_recv.at[k, 0], (dp_x, seq)),
                send(to_y, to_y, f_send.at[k, 1], f_recv.at[k, 1], (dp_y, seq))]

    def second_copies(own, full, rows, cols, k):
        low, high = pl.ds(0, rows // 2), pl.ds(rows // 2, rows // 2)
        to_y = full.at[y, :, :, c, low, cols]
        to_x = full.at[:, x, :, c, high, cols]
        return [send(to_y, to_y, s_send.at[k, 0], s_recv.at[k, 0], (dp_y, seq)),
                send(to_x, to_x, s_send.at[k, 1], s_recv.at[k, 1], (dp_x, seq))]

    def core_copies(own, full, rows, cols, k):
        part = full.at[:, :, :, c, :, cols]
        return [send(part, part, c_send.at[k], c_recv.at[k], (dp, 2 * z + (1 - c)))]

    def away_copies(k):
        copies = []
        for step in range(1, 8):
            peer = (seq + step) % 8
            copies.append(send(
                qkv.at[k, pl.ds(pl.multiple_of(peer * share, 16), share)],
                col.at[k, pl.ds(pl.multiple_of(seq * share, 16), share)],
                a_send.at[k, step - 1], a_recv.at[k, step - 1], (dp, peer)))
        return copies

    def back_copies(k):
        copies = []
        for step in range(1, 8):
            peer = (seq + step) % 8
            copies.append(send(
                col_out.at[k, pl.ds(pl.multiple_of(peer * share, 16), share)],
                home.at[k, pl.ds(pl.multiple_of(seq * share, 16), share)],
                b_send.at[k, step - 1], b_recv.at[k, step - 1], (dp, peer)))
        return copies

    def job(make, k, act):
        @pl.when((k >= 0) & (k < HEADS))
        def _():
            cols = pl.ds(pl.multiple_of(((k + HALF) % HEADS) * PACK, 128), PACK)
            for copy in make(wq_ref, w, wq_ref.shape[0], cols, k):
                act(copy)

        @pl.when((k >= HEADS) & (k < JOBS))
        def _():
            cols = pl.ds(pl.multiple_of((k - HEADS) * chunk, 128), chunk)
            for copy in make(wo_ref, wo, wo_ref.shape[0], cols, k):
                act(copy)

    def start(copy):
        copy.start()

    def arrived(copy):
        copy.wait_recv()

    def sent(copy):
        copy.wait_send()

    def attention(packed, bias):
        query, keys, values = (packed[:, p * HEAD_DIM:(p + 1) * HEAD_DIM] for p in range(3))
        scores = lax.dot_general(query, keys, (((1,), (1,)), ((), ())),
                                 preferred_element_type=jnp.float32)
        scores = scores * (1.0 / math.sqrt(HEAD_DIM)) + bias.astype(jnp.float32)
        expo = jnp.exp(scores - jnp.max(scores, axis=-1, keepdims=True))
        weights = expo * (1.0 / jnp.sum(expo, axis=-1, keepdims=True))
        return jnp.dot(weights.astype(jnp.bfloat16), values,
                       preferred_element_type=jnp.float32).astype(jnp.bfloat16)

    def reorder(order, block):
        return jnp.dot(order, block, preferred_element_type=jnp.float32).astype(jnp.bfloat16)

    def z_ahead(t):
        z_job(1, t + 3, start, z_sends)
        z_job(1, t + 2, arrived, z_receives)
        z_job(2, t + 2, start, z_sends)
        z_job(2, t + 1, arrived, z_receives)
        z_job(3, t + 1, start, z_sends)

    z_job(1, jnp.int32(0), start, z_sends)
    z_job(1, jnp.int32(1), start, z_sends)
    for copy in local:
        copy.wait()

    def permute(i, _):
        cols = pl.ds(pl.multiple_of(i * 512, 128), 512)
        xp[:, cols] = reorder(perm_ref[...], x_ref[:, cols])
        return 0

    z_job(1, jnp.int32(0), arrived, z_receives)
    z_job(2, jnp.int32(0), start, z_sends)
    z_job(1, jnp.int32(2), start, z_sends)
    z_job(1, jnp.int32(1), arrived, z_receives)
    z_job(2, jnp.int32(1), start, z_sends)
    z_job(2, jnp.int32(0), arrived, z_receives)
    z_job(3, jnp.int32(0), start, z_sends)
    lax.fori_loop(0, width // 512, permute, 0)

    def body(t, _):
        z_job(3, t - 1, arrived, z_receives)
        job(first_copies, t - 1, start)
        job(first_copies, t - 2, arrived)
        job(second_copies, t - 2, start)
        job(second_copies, t - 5, arrived)
        job(core_copies, t - 5, start)
        z_ahead(t)
        job(core_copies, t - 6, arrived)
        k = t - 6

        @pl.when((k >= 0) & (k < HEADS))
        def _():
            cols = pl.ds(pl.multiple_of(((k + HALF) % HEADS) * PACK, 128), PACK)
            weight = w[:, :, :, :, :, cols].reshape(xp.shape[1], PACK)
            qkv[k] = jnp.dot(xp[...], weight,
                             preferred_element_type=jnp.float32).astype(jnp.bfloat16)

            @pl.when(k < HALF)
            def _():
                for copy in away_copies(k):
                    copy.start()
                mine = pl.ds(pl.multiple_of(seq * share, 16), share)
                col[k, mine] = qkv[k, mine]

            @pl.when(k >= HALF)
            def _():
                result = attention(qkv[k], bias_ref[0])
                heads[:, pl.ds(pl.multiple_of((k - HALF) * HEAD_DIM, 128), HEAD_DIM)] = reorder(
                    unperm_ref[...], result)

        a = t - 9

        @pl.when((a >= 0) & (a < HALF))
        def _():
            for copy in away_copies(a):
                copy.wait_recv()
            col_out[a] = attention(col[a], bias_ref[1])
            for copy in back_copies(a):
                copy.start()
            mine = pl.ds(pl.multiple_of(seq * share, 16), share)
            home[a, mine] = col_out[a, mine]

        b = t - 11

        @pl.when((b >= 0) & (b < HALF))
        def _():
            for copy in back_copies(b):
                copy.wait_recv()
            heads[:, pl.ds(pl.multiple_of((b + HALF) * HEAD_DIM, 128), HEAD_DIM)] = reorder(
                unperm_ref[...], home[b])

        @pl.when((k >= HEADS) & (k < JOBS))
        def _():
            cols = pl.ds(pl.multiple_of((k - HEADS) * chunk, 128), chunk)
            weight = wo[:, :, :, :, :, cols].reshape(heads.shape[1], chunk)
            out_ref[:, cols] = jnp.dot(heads[...], weight,
                                       preferred_element_type=jnp.float32).astype(jnp.bfloat16)
        return 0

    lax.fori_loop(0, JOBS + 6, body, 0)

    def drain(k, _):
        for hop in (1, 2, 3):
            z_job(hop, k, sent, z_sends)
        for make in (first_copies, second_copies, core_copies):
            job(make, k, sent)
        return 0

    lax.fori_loop(0, JOBS, drain, 0)

    def drain_heads(k, _):
        for copy in away_copies(k) + back_copies(k):
            copy.wait_send()
        return 0

    lax.fori_loop(0, HALF, drain_heads, 0)


def on_torus(tokens, w_qkv, w_out):
    _, count, width = tokens.shape
    rows, share = count // COLS, COLS // 8
    places = np.arange(count).reshape(rows, 8, share).transpose(1, 0, 2).reshape(count)
    perm = (places[:, None] == np.arange(count)[None, :])
    later = np.arange(count)[:, None] >= np.arange(count)[None, :]
    in_row = (places // COLS)[:, None] == (places // COLS)[None, :]
    in_col = (np.arange(count) % share)[:, None] == (np.arange(count) % share)[None, :]
    bias = np.where(np.stack([in_row & later, in_col & later]), 0.0, -np.inf)
    bf16 = jnp.bfloat16
    inner = HEADS * HEAD_DIM
    vmem = pl.BlockSpec(memory_space=pltpu.VMEM)
    dma = pltpu.SemaphoreType.DMA
    out = pl.pallas_call(
        functools.partial(fused, count, width),
        out_shape=jax.ShapeDtypeStruct((count, width), bf16),
        in_specs=[pl.BlockSpec(memory_space=pltpu.HBM)] * 6,
        out_specs=vmem,
        scratch_shapes=[
            pltpu.VMEM((count, width), bf16),
            pltpu.VMEM((count, count), bf16),
            pltpu.VMEM((count, count), bf16),
            pltpu.VMEM((2, count, count), bf16),
            dma((6,)),
            pltpu.VMEM((count, width), bf16),
            pltpu.VMEM((2, 2, 4, 2) + w_qkv.shape, bf16),
            pltpu.VMEM((2, 2, 4, 2) + w_out.shape, bf16),
            pltpu.VMEM((HEADS, count, PACK), bf16),
            pltpu.VMEM((HALF, count, PACK), bf16),
            pltpu.VMEM((HALF, count, HEAD_DIM), bf16),
            pltpu.VMEM((HALF, count, HEAD_DIM), bf16),
            pltpu.VMEM((count, inner), bf16),
            dma((JOBS, 6)), dma((JOBS, 6)),
            dma((JOBS, 2)), dma((JOBS, 2)),
            dma((JOBS, 2)), dma((JOBS, 2)),
            dma((JOBS,)), dma((JOBS,)),
            dma((HALF, 7)), dma((HALF, 7)),
            dma((HALF, 7)), dma((HALF, 7)),
        ],
        compiler_params=pltpu.CompilerParams(
            collective_id=0, has_side_effects=True, vmem_limit_bytes=62 * 2**20),
        cost_estimate=pl.CostEstimate(
            flops=2 * count * width * (HEADS * PACK + inner),
            bytes_accessed=4 * count * width, transcendentals=HEADS * count * count),
    )(tokens.reshape(count, width), w_qkv, w_out, jnp.asarray(perm, bf16),
      jnp.asarray(perm.T, bf16), jnp.asarray(bias, bf16))
    return out.reshape(tokens.shape)


def solution(mesh):
    in_specs = (P("dp", "seq", None), P(("dp", "seq"), None), P(("dp", "seq"), None))
    out_specs = P("dp", "seq", None)
    fits = mesh.shape["dp"] == 4 and mesh.shape["seq"] == 8
    return jax.shard_map(
        on_torus if fits else on_device,
        mesh=mesh, in_specs=in_specs, out_specs=out_specs, check_vma=False
    )
```

```python
import functools
import math

import jax
import jax.numpy as jnp
import numpy as np
from jax import lax
from jax.experimental import pallas as pl
from jax.experimental.pallas import tpu as pltpu
from jax.sharding import PartitionSpec as P

HEADS = 8
HEAD_DIM = 128
COLS = 96


def attend(query, keys, values, allowed):
    scores = jnp.einsum(
        "shqd,shkd->shqk", query, keys, preferred_element_type=jnp.float32
    ) / math.sqrt(query.shape[-1])
    scores = jnp.where(allowed, scores, -jnp.inf)
    top = jnp.max(scores, axis=-1, keepdims=True)
    expo = jnp.exp(scores - top)
    weights = (expo / jnp.sum(expo, axis=-1, keepdims=True)).astype(jnp.bfloat16)
    return jnp.einsum(
        "shqk,shkd->shqd", weights, values, preferred_element_type=jnp.float32
    ).astype(jnp.bfloat16)


def add_rows(left, piece):
    return jnp.dot(left, piece, preferred_element_type=jnp.float32)


def column_heads(packed):
    seq_count, grid_rows, local_cols, count, width = packed.shape
    length = grid_rows * local_cols
    flat = packed.reshape(seq_count, length, count, 3, width // 3)
    flat = jnp.transpose(flat, (0, 2, 3, 1, 4))
    places = jnp.arange(length)
    allowed = (places[:, None] % local_cols == places[None, :] % local_cols) & (
        places[:, None] >= places[None, :]
    )
    result = attend(flat[:, :, 0], flat[:, :, 1], flat[:, :, 2], allowed)
    result = jnp.transpose(result, (0, 2, 1, 3)).reshape(
        seq_count, grid_rows, local_cols, count, width // 3
    )
    return lax.all_to_all(result, "seq", split_axis=1, concat_axis=2, tiled=True)


def on_device(tokens, w_qkv, w_out):
    seq_count, tok_count, width = tokens.shape
    flat = tokens.reshape(seq_count * tok_count, width)
    half = HEADS // 2
    qkv = add_rows(flat, lax.all_gather(w_qkv, ("dp", "seq"), axis=0, tiled=True))
    qkv = qkv.astype(jnp.bfloat16).reshape(seq_count, tok_count, HEADS, 3, HEAD_DIM)
    col_packed = qkv[:, :, half:].reshape(seq_count, tok_count // COLS, COLS, half, 3 * HEAD_DIM)
    col_out = column_heads(
        lax.all_to_all(col_packed, "seq", split_axis=2, concat_axis=1, tiled=True)
    )
    col_out = col_out.reshape(seq_count, tok_count, half, HEAD_DIM)
    row_part = jnp.transpose(qkv[:, :, :half], (0, 2, 3, 1, 4))
    places = jnp.arange(tok_count)
    row_mask = (places[:, None] // COLS == places[None, :] // COLS) & (
        places[:, None] >= places[None, :]
    )
    row_out = attend(row_part[:, :, 0], row_part[:, :, 1], row_part[:, :, 2], row_mask)
    row_out = jnp.transpose(row_out, (0, 2, 1, 3))
    heads_out = jnp.concatenate([row_out, col_out], axis=2).reshape(
        seq_count * tok_count, HEADS * HEAD_DIM
    )
    mixed = add_rows(heads_out, lax.all_gather(w_out, ("dp", "seq"), axis=0, tiled=True))
    return mixed.astype(jnp.bfloat16).reshape(seq_count, tok_count, w_out.shape[1])


HALF = HEADS // 2
PACK = 3 * HEAD_DIM
OUT_CHUNKS = 8
JOBS = HEADS + OUT_CHUNKS
MESH = pl.DeviceIdType.MESH


def fused(tok_count, width, x_hbm, wq_ref, wo_ref, perm_hbm, unperm_hbm, bias_hbm, out_ref,
          x_ref, perm_ref, unperm_ref, bias_ref, l_sem, xp, w, wo, qkv, col, col_out, home, heads,
          z_send, z_recv, f_send, f_recv, s_send, s_recv, c_send, c_recv,
          a_send, a_recv, b_send, b_recv):
    dp, seq = lax.axis_index("dp"), lax.axis_index("seq")
    y, x = dp // 2, dp % 2
    z, c = seq // 2, seq % 2
    dp_x, dp_y = 2 * y + (1 - x), 2 * (1 - y) + x
    share = tok_count // 8
    chunk = width // OUT_CHUNKS

    local = [pltpu.make_async_copy(source, target, l_sem.at[i]) for i, (source, target) in
             enumerate(((x_hbm, x_ref), (wq_ref, w.at[y, x, z, c]), (wo_ref, wo.at[y, x, z, c]),
                        (perm_hbm, perm_ref), (unperm_hbm, unperm_ref), (bias_hbm, bias_ref)))]
    for copy in local:
        copy.start()

    barrier = pltpu.get_barrier_semaphore()
    for step in range(1, 8):
        pl.semaphore_signal(barrier, inc=1, device_id=(dp, (seq + step) % 8), device_id_type=MESH)
    for other in (dp_x, dp_y):
        pl.semaphore_signal(barrier, inc=1, device_id=(other, seq), device_id_type=MESH)
    pl.semaphore_wait(barrier, 9)

    def send(source, target, s_sem, r_sem, device):
        return pltpu.make_async_remote_copy(
            src_ref=source, dst_ref=target, send_sem=s_sem, recv_sem=r_sem,
            device_id=device, device_id_type=MESH)

    def z_copies(hop, own, full, rows, cols, k):
        below, above = (z + 5 - hop) % 4, (z + hop - 1) % 4
        up, down = (z + 1) % 4, (z + 3) % 4
        copies = []
        for way, (block, target) in enumerate(((below, up), (above, down))):
            landing = full.at[y, x, block, c, :, cols]
            slot = 3 * way + hop - 1
            copies.append(send(own.at[:, cols] if hop == 1 else landing, landing,
                               z_send.at[k, slot], z_recv.at[k, slot], (dp, 2 * target + c)))
        return copies

    def z_sends(hop):
        return [(z < 3) & (z >= hop - 1), (z > 0) & (z <= 4 - hop)]

    def z_receives(hop):
        return [z >= hop, z <= 3 - hop]

    def z_job(hop, k, act, conditions):
        def guarded(own, full, rows, cols, k):
            return list(zip(conditions(hop), z_copies(hop, own, full, rows, cols, k)))

        def run(pair):
            condition, copy = pair

            @pl.when(condition)
            def _():
                act(copy)

        job(guarded, k, run)

    def first_copies(own, full, rows, cols, k):
        low, high = pl.ds(0, rows // 2), pl.ds(rows // 2, rows // 2)
        to_x = full.at[y, x, :, c, low, cols]
        to_y = full.at[y, x, :, c, high, cols]
        return [send(to_x, to_x, f_send.at[k, 0], f_recv.at[k, 0], (dp_x, seq)),
                send(to_y, to_y, f_send.at[k, 1], f_recv.at[k, 1], (dp_y, seq))]

    def second_copies(own, full, rows, cols, k):
        low, high = pl.ds(0, rows // 2), pl.ds(rows // 2, rows // 2)
        to_y = full.at[y, :, :, c, low, cols]
        to_x = full.at[:, x, :, c, high, cols]
        return [send(to_y, to_y, s_send.at[k, 0], s_recv.at[k, 0], (dp_y, seq)),
                send(to_x, to_x, s_send.at[k, 1], s_recv.at[k, 1], (dp_x, seq))]

    def core_copies(own, full, rows, cols, k):
        part = full.at[:, :, :, c, :, cols]
        return [send(part, part, c_send.at[k], c_recv.at[k], (dp, 2 * z + (1 - c)))]

    def away_copies(k):
        copies = []
        for step in range(1, 8):
            peer = (seq + step) % 8
            copies.append(send(
                qkv.at[k, pl.ds(pl.multiple_of(peer * share, 16), share)],
                col.at[k, pl.ds(pl.multiple_of(seq * share, 16), share)],
                a_send.at[k, step - 1], a_recv.at[k, step - 1], (dp, peer)))
        return copies

    def back_copies(k):
        copies = []
        for step in range(1, 8):
            peer = (seq + step) % 8
            copies.append(send(
                col_out.at[k, pl.ds(pl.multiple_of(peer * share, 16), share)],
                home.at[k, pl.ds(pl.multiple_of(seq * share, 16), share)],
                b_send.at[k, step - 1], b_recv.at[k, step - 1], (dp, peer)))
        return copies

    def job(make, k, act):
        @pl.when((k >= 0) & (k < HEADS))
        def _():
            cols = pl.ds(pl.multiple_of(((k + HALF) % HEADS) * PACK, 128), PACK)
            for copy in make(wq_ref, w, wq_ref.shape[0], cols, k):
                act(copy)

        @pl.when((k >= HEADS) & (k < JOBS))
        def _():
            cols = pl.ds(pl.multiple_of((k - HEADS) * chunk, 128), chunk)
            for copy in make(wo_ref, wo, wo_ref.shape[0], cols, k):
                act(copy)

    def start(copy):
        copy.start()

    def arrived(copy):
        copy.wait_recv()

    def sent(copy):
        copy.wait_send()

    def attention(packed, bias):
        query, keys, values = (packed[:, p * HEAD_DIM:(p + 1) * HEAD_DIM] for p in range(3))
        scores = lax.dot_general(query, keys, (((1,), (1,)), ((), ())),
                                 preferred_element_type=jnp.float32)
        scores = scores * (1.0 / math.sqrt(HEAD_DIM)) + bias.astype(jnp.float32)
        expo = jnp.exp(scores - jnp.max(scores, axis=-1, keepdims=True))
        weights = expo * (1.0 / jnp.sum(expo, axis=-1, keepdims=True))
        return jnp.dot(weights.astype(jnp.bfloat16), values,
                       preferred_element_type=jnp.float32).astype(jnp.bfloat16)

    def reorder(order, block):
        return jnp.dot(order, block, preferred_element_type=jnp.float32).astype(jnp.bfloat16)

    def z_ahead(t):
        z_job(1, t + 3, start, z_sends)
        z_job(1, t + 2, arrived, z_receives)
        z_job(2, t + 2, start, z_sends)
        z_job(2, t + 1, arrived, z_receives)
        z_job(3, t + 1, start, z_sends)

    z_job(1, jnp.int32(0), start, z_sends)
    z_job(1, jnp.int32(1), start, z_sends)
    for copy in local:
        copy.wait()

    def permute(i, _):
        cols = pl.ds(pl.multiple_of(i * 512, 128), 512)
        xp[:, cols] = reorder(perm_ref[...], x_ref[:, cols])
        return 0

    z_job(1, jnp.int32(0), arrived, z_receives)
    z_job(2, jnp.int32(0), start, z_sends)
    z_job(1, jnp.int32(2), start, z_sends)
    z_job(1, jnp.int32(1), arrived, z_receives)
    z_job(2, jnp.int32(1), start, z_sends)
    z_job(2, jnp.int32(0), arrived, z_receives)
    z_job(3, jnp.int32(0), start, z_sends)
    lax.fori_loop(0, width // 512, permute, 0)

    def body(t, _):
        z_job(3, t - 1, arrived, z_receives)
        job(first_copies, t - 1, start)
        job(first_copies, t - 2, arrived)
        job(second_copies, t - 2, start)
        job(second_copies, t - 5, arrived)
        job(core_copies, t - 5, start)
        z_ahead(t)
        job(core_copies, t - 6, arrived)
        k = t - 6

        @pl.when((k >= 0) & (k < HEADS))
        def _():
            cols = pl.ds(pl.multiple_of(((k + HALF) % HEADS) * PACK, 128), PACK)
            weight = w[:, :, :, :, :, cols].reshape(xp.shape[1], PACK)
            qkv[k] = jnp.dot(xp[...], weight,
                             preferred_element_type=jnp.float32).astype(jnp.bfloat16)

            @pl.when(k < HALF)
            def _():
                for copy in away_copies(k):
                    copy.start()
                mine = pl.ds(pl.multiple_of(seq * share, 16), share)
                col[k, mine] = qkv[k, mine]

            @pl.when(k >= HALF)
            def _():
                result = attention(qkv[k], bias_ref[0])
                heads[:, pl.ds(pl.multiple_of((k - HALF) * HEAD_DIM, 128), HEAD_DIM)] = reorder(
                    unperm_ref[...], result)

        a = t - 9

        @pl.when((a >= 0) & (a < HALF))
        def _():
            for copy in away_copies(a):
                copy.wait_recv()
            col_out[a] = attention(col[a], bias_ref[1])
            for copy in back_copies(a):
                copy.start()
            mine = pl.ds(pl.multiple_of(seq * share, 16), share)
            home[a, mine] = col_out[a, mine]

        b = t - 11

        @pl.when((b >= 0) & (b < HALF))
        def _():
            for copy in back_copies(b):
                copy.wait_recv()
            heads[:, pl.ds(pl.multiple_of((b + HALF) * HEAD_DIM, 128), HEAD_DIM)] = reorder(
                unperm_ref[...], home[b])

        @pl.when((k >= HEADS) & (k < JOBS))
        def _():
            cols = pl.ds(pl.multiple_of((k - HEADS) * chunk, 128), chunk)
            weight = wo[:, :, :, :, :, cols].reshape(heads.shape[1], chunk)
            out_ref[:, cols] = jnp.dot(heads[...], weight,
                                       preferred_element_type=jnp.float32).astype(jnp.bfloat16)
        return 0

    lax.fori_loop(0, JOBS + 6, body, 0)

    def drain(k, _):
        for hop in (1, 2, 3):
            z_job(hop, k, sent, z_sends)
        for make in (first_copies, second_copies, core_copies):
            job(make, k, sent)
        return 0

    lax.fori_loop(0, JOBS, drain, 0)

    def drain_heads(k, _):
        for copy in away_copies(k) + back_copies(k):
            copy.wait_send()
        return 0

    lax.fori_loop(0, HALF, drain_heads, 0)


def on_torus(tokens, w_qkv, w_out):
    _, count, width = tokens.shape
    rows, share = count // COLS, COLS // 8
    places = np.arange(count).reshape(rows, 8, share).transpose(1, 0, 2).reshape(count)
    perm = (places[:, None] == np.arange(count)[None, :])
    later = np.arange(count)[:, None] >= np.arange(count)[None, :]
    in_row = (places // COLS)[:, None] == (places // COLS)[None, :]
    in_col = (np.arange(count) % share)[:, None] == (np.arange(count) % share)[None, :]
    bias = np.where(np.stack([in_row & later, in_col & later]), 0.0, -np.inf)
    bf16 = jnp.bfloat16
    inner = HEADS * HEAD_DIM
    vmem = pl.BlockSpec(memory_space=pltpu.VMEM)
    dma = pltpu.SemaphoreType.DMA
    out = pl.pallas_call(
        functools.partial(fused, count, width),
        out_shape=jax.ShapeDtypeStruct((count, width), bf16),
        in_specs=[pl.BlockSpec(memory_space=pltpu.HBM)] * 6,
        out_specs=vmem,
        scratch_shapes=[
            pltpu.VMEM((count, width), bf16),
            pltpu.VMEM((count, count), bf16),
            pltpu.VMEM((count, count), bf16),
            pltpu.VMEM((2, count, count), bf16),
            dma((6,)),
            pltpu.VMEM((count, width), bf16),
            pltpu.VMEM((2, 2, 4, 2) + w_qkv.shape, bf16),
            pltpu.VMEM((2, 2, 4, 2) + w_out.shape, bf16),
            pltpu.VMEM((HEADS, count, PACK), bf16),
            pltpu.VMEM((HALF, count, PACK), bf16),
            pltpu.VMEM((HALF, count, HEAD_DIM), bf16),
            pltpu.VMEM((HALF, count, HEAD_DIM), bf16),
            pltpu.VMEM((count, inner), bf16),
            dma((JOBS, 6)), dma((JOBS, 6)),
            dma((JOBS, 2)), dma((JOBS, 2)),
            dma((JOBS, 2)), dma((JOBS, 2)),
            dma((JOBS,)), dma((JOBS,)),
            dma((HALF, 7)), dma((HALF, 7)),
            dma((HALF, 7)), dma((HALF, 7)),
        ],
        compiler_params=pltpu.CompilerParams(
            collective_id=0, has_side_effects=True, vmem_limit_bytes=62 * 2**20),
        cost_estimate=pl.CostEstimate(
            flops=2 * count * width * (HEADS * PACK + inner),
            bytes_accessed=4 * count * width, transcendentals=HEADS * count * count),
    )(tokens.reshape(count, width), w_qkv, w_out, jnp.asarray(perm, bf16),
      jnp.asarray(perm.T, bf16), jnp.asarray(bias, bf16))
    return out.reshape(tokens.shape)


def solution(mesh):
    in_specs = (P("dp", "seq", None), P(("dp", "seq"), None), P(("dp", "seq"), None))
    out_specs = P("dp", "seq", None)
    fits = mesh.shape["dp"] == 4 and mesh.shape["seq"] == 8
    return jax.shard_map(
        on_torus if fits else on_device,
        mesh=mesh, in_specs=in_specs, out_specs=out_specs, check_vma=False
    )
```
